256 devices in a mesh: island: 32 (over z, x), fsdp: 8 (over y, core).
Axes of the slice: x: 4, y: 4, z: 8, core: 2. Of those that a mesh axis runs over, the one named last changes fastest.
Arguments:
- gradient: bfloat16 [32, 2560, 4096], P('island', 'fsdp'), may hold values from -300 to 300, as said below
- momentum: bfloat16 [32, 2560, 4096], P('island', 'fsdp'), may hold values from -300 to 300, as said below
- drift: float32 [32, 2560, 4096], P('island', 'fsdp'), may hold values from -6 to 6
- outer_weights: float32 [2560, 4096], P('fsdp', 'island'), may hold values from -6 to 6
- outer_momentum: float32 [2560, 4096], P('fsdp', 'island'), may hold values from -6 to 6
Outputs:
- new_weights: float32 [2560, 4096], P('fsdp', 'island')
- new_momentum: float32 [2560, 4096], P('fsdp', 'island')
The draws below stay inside these ranges and needn't reach their ends.
Inputs may be any that keep to these rules, and one draw needn't show every extreme that they name: `gradient`: real values. `momentum`: real values.
All inputs are finite; a program needn't handle non-finite values.
Results may differ from the reference program's by a relative error of at most 0.00075.
Values may be sent and summed in bfloat16 or wider, within the bound.
A program may use at most 64 MiB of HBM per device.

```python
import math
import jax
import jax.numpy as jnp
from jax import lax

ROWS = 2560
BLK = 512
NS_STEPS = 2
COLS = 4096
ISLANDS = 32


def shared_scales(key):
    row_key, col_key = jax.random.split(key)
    row_frac = jnp.arange(ROWS, dtype=jnp.float32) / ROWS
    row_scale = 10.0 ** (0.5 * row_frac + 0.5 * jax.random.uniform(row_key, (ROWS,), jnp.float32))
    col_scale = 10.0 ** jax.random.uniform(col_key, (COLS,), jnp.float32)
    return (row_scale, col_scale)


def scaled_values(key, row_scale, col_scale):
    shape = (ISLANDS, ROWS, COLS)
    base = jax.random.normal(key, shape, jnp.float32)
    return 0.3 * base * row_scale[None, :, None] * col_scale[None, None, :]


def draw_gradient(key, part):
    row_scale, col_scale = shared_scales(key)
    key = jax.random.fold_in(key, 11)
    return scaled_values(key, row_scale, col_scale).astype(jnp.bfloat16)


def draw_momentum(key, part):
    row_scale, col_scale = shared_scales(key)
    key = jax.random.fold_in(key, 12)
    return scaled_values(key, row_scale, col_scale).astype(jnp.bfloat16)


def raised(drawn, stream_key, source, target, blocks, factor):
    owner, partner = [(jnp.arange(drawn.shape[position]) // (drawn.shape[position] // blocks)).reshape([-1 if axis == position else 1 for axis in range(drawn.ndim)]) for position in (source, target)]
    chosen = jax.random.permutation(stream_key, blocks)[partner]
    strong = (owner == chosen) | (owner == (partner + blocks // 2) % blocks)
    return jnp.where(strong, factor * drawn, drawn)


def block_levels(key, extent, shards, smallest, largest):
    def one(position, parts):
        heights = jax.random.uniform(jax.random.fold_in(jax.random.fold_in(key, 6), position), (parts,), jnp.float32, smallest / len(shards), largest / len(shards))
        return jnp.repeat(jnp.exp(heights), extent[position] // parts).reshape((-1,) + (1,) * (len(extent) - position - 1))

    gain = one(*shards[0])
    for cut in shards[1:]:
        gain = gain * one(*cut)
    return gain


def bell_draw(own_key, shape, spread, most, cuts=(), kind=jnp.bfloat16):
    drawn = spread * jax.random.normal(own_key, shape, jnp.float32)
    if cuts:
        drawn = drawn * block_levels(own_key, shape, cuts, -0.22, 0.18)
    return jnp.clip(drawn, -most, most).astype(kind)


def noise_with(stream_key, dims, scale, reach, pieces, heavy, kind=jnp.bfloat16):
    values = scale * jax.random.normal(stream_key, dims, jnp.float32)
    if pieces:
        values = values * block_levels(stream_key, dims, pieces, -0.22, 0.18)
    return jnp.clip(raised(values, jax.random.fold_in(stream_key, 3), *heavy), -reach, reach).astype(kind)


def setup_inputs(seed: int = 0) -> dict:
    streams_of = jax.random.split(jax.random.key(seed), 6)
    return {
        "gradient": draw_gradient(jax.random.fold_in(streams_of[5], 71), 0),
        "momentum": draw_momentum(jax.random.fold_in(streams_of[5], 71), 0),
        "drift": noise_with(streams_of[2], (ISLANDS, ROWS, COLS), 1.0, 6.0, ((0, 32), (1, 8)), (0, 2, 32, 2.75), jnp.float32),
        "outer_weights": bell_draw(streams_of[3], (ROWS, COLS), 1.0, 6.0, ((0, 8), (1, 32)), jnp.float32),
        "outer_momentum": bell_draw(streams_of[4], (ROWS, COLS), 0.5, 6.0, ((0, 8), (1, 32)), jnp.float32),
    }


EPS = 1e-07
COEF_A = 3.4445
COEF_B = -4.775
COEF_C = 2.0315
BETA = 0.95
OUTER_BETA = 0.9
OUTER_LR = 0.7

def orthogonalize(block):
    norm_value = jnp.sqrt(jnp.sum(block * block))
    current = (block / (norm_value + EPS)).astype(jnp.bfloat16)
    for sweep in range(NS_STEPS):
        gram = lax.dot_general(current, current, (((0,), (0,)), ((), ())), preferred_element_type=jnp.float32).astype(jnp.bfloat16)
        square = jnp.dot(gram, gram, preferred_element_type=jnp.float32)
        poly = (COEF_B * gram.astype(jnp.float32) + COEF_C * square).astype(jnp.bfloat16)
        current = (COEF_A * current.astype(jnp.float32) + jnp.dot(current, poly, preferred_element_type=jnp.float32)).astype(jnp.bfloat16)
    return current

def reference(gradient, momentum, drift, outer_weights, outer_momentum):
    step_scale = 0.2 * math.sqrt(max(ROWS, BLK))
    groups = COLS // BLK

    def replica(total, inputs):
        grad_one, mom_one, drift_one = inputs
        grad_f = grad_one.astype(jnp.float32)
        nesterov_in = grad_f + BETA * (BETA * mom_one.astype(jnp.float32) + grad_f)
        blocks = nesterov_in.reshape(ROWS, groups, BLK).transpose(1, 0, 2)
        orth = lax.map(orthogonalize, blocks)
        update = orth.transpose(1, 0, 2).reshape(ROWS, COLS)
        return (total + drift_one + step_scale * update.astype(jnp.float32), None)
    total, unused = lax.scan(replica, jnp.zeros((ROWS, COLS), jnp.float32), (gradient, momentum, drift))
    pseudo = total / ISLANDS
    new_momentum = OUTER_BETA * outer_momentum + pseudo
    new_weights = outer_weights - OUTER_LR * (pseudo + OUTER_BETA * new_momentum)
    return (new_weights, new_momentum)
```

```python
import functools
import math

import jax
import jax.numpy as jnp
from jax import lax
from jax.experimental import pallas as pl
from jax.experimental.pallas import tpu as pltpu
from jax.sharding import PartitionSpec as P

ROWS = 2560
BLK = 512
EPS = 1e-07
COEF_A = 3.4445
COEF_B = -4.775
COEF_C = 2.0315
BETA = 0.95
OUTER_BETA = 0.9
OUTER_LR = 0.7
STEP_SCALE = 0.2 * math.sqrt(max(ROWS, BLK))

MESH = pl.DeviceIdType.MESH
F32 = jnp.float32
BF16 = jnp.bfloat16
NZ, NX, NY = 8, 4, 4
NF = 2 * NY
LANES = 128
GROUPS = ((4, 3), (5, 2), (6, 1), (7, 0))
SENDS = tuple((dy, core) for core in (0, 1) for dy in (2, 1, 3, 0))
CODE1, CODE2, CODE4 = 14.0, 7.0, 3.5
STEP_ROWS = 64


def code(v, c):
    return jnp.exp(v * c).astype(BF16)


def decode(y, c):
    return jnp.log(y.astype(F32)) * (1.0 / c)


def plain(v, c):
    return v.astype(BF16)


def unplain(y, c):
    return y.astype(F32)


def kernel(
    g_hbm, m_hbm, d_hbm, ow_ref, om_ref, nw_ref, nm_ref,
    gbuf, mbuf, dbuf, xs, xr, gram,
    de, dd2, dl1, dr1, dzs, dzr, dacc,
    oe, od2, ol1, or1, ozs, ozr, oacc, tsend, trecv,
    load_sem, ysend, yrecv,
    d2send, d2recv, d1send, d1recv, dzsend, dzrecv,
    o2send, o2recv, o1send, o1recv, ozsend, ozrecv, tsem,
):
    isl = lax.axis_index("island")
    f = lax.axis_index("fsdp")
    z, x = isl // NX, isl % NX
    y, core = f // 2, f % 2
    rows = g_hbm.shape[1]
    chunks = rows // STEP_ROWS
    right = (z * NX + (x + 1) % NX, f)
    left = (z * NX + (x + NX - 1) % NX, f)
    x_right, x_left, x_far = (x + 1) % NX, (x + NX - 1) % NX, (x + 2) % NX
    swap = (f * NX + x, z)

    def at_fsdp(dy, c):
        return ((y + dy) % NY) * 2 + c

    barrier = pltpu.get_barrier_semaphore()

    def greet(dev):
        pl.semaphore_signal(barrier, inc=1, device_id=dev, device_id_type=MESH)

    for d in range(1, NF):
        greet((isl, (f + d) % NF))
    for d in range(1, NZ):
        greet((((z + d) % NZ) * NX + x, f))
    greet(right)
    greet(left)

    @pl.when(z != f)
    def _():
        greet(swap)

    def g_load(j):
        cols = pl.ds(pl.multiple_of(at_fsdp(*SENDS[j]) * BLK, BLK), BLK)
        return (
            pltpu.make_async_copy(g_hbm.at[0, :, cols], gbuf.at[j], load_sem.at[j]),
            pltpu.make_async_copy(m_hbm.at[0, :, cols], mbuf.at[j], load_sem.at[NF + j]),
        )

    def d_load(k):
        cols = pl.ds(pl.multiple_of(((z + k) % NZ) * BLK, BLK), BLK)
        return pltpu.make_async_copy(d_hbm.at[0, :, cols], dbuf.at[k], load_sem.at[2 * NF + k])

    for j in range(NF):
        for copy in g_load(j):
            copy.start()
    for group in GROUPS:
        for k in group:
            d_load(k).start()

    pl.semaphore_wait(barrier, NF - 1 + NZ - 1 + 2 + jnp.where(z != f, 1, 0))

    def y_copy(j):
        dest = at_fsdp(*SENDS[j])
        return pltpu.make_async_remote_copy(
            src_ref=xs.at[j], dst_ref=xr.at[f], send_sem=ysend.at[j], recv_sem=yrecv.at[f],
            device_id=(isl, dest), device_id_type=MESH,
        )

    for j in range(NF):
        for copy in g_load(j):
            copy.wait()
        dy, c = SENDS[j]

        def nesterov(dst):
            @pl.loop(0, chunks)
            def _(i):
                r = pl.ds(pl.multiple_of(i * STEP_ROWS, STEP_ROWS), STEP_ROWS)
                grad = gbuf[j, r, :].astype(F32)
                mom = mbuf[j, r, :].astype(F32)
                dst[r, :] = (grad + BETA * (BETA * mom + grad)).astype(BF16)

        if dy:
            nesterov(xs.at[j])
            y_copy(j).start()
        else:
            @pl.when(core == c)
            def _():
                nesterov(xr.at[f])

            @pl.when(core != c)
            def _():
                nesterov(xs.at[j])
                y_copy(j).start()

    def reduction(enc, dec, c1, c2, c4, e, d2, l1, r1, zs, zr, acc, own, s2, v2, s1, v1, sz, vz):
        def rc(src, dst, ss, rs, dev):
            return pltpu.make_async_remote_copy(
                src_ref=src, dst_ref=dst, send_sem=ss, recv_sem=rs, device_id=dev, device_id_type=MESH
            )

        def far(k, to_right):
            return rc(e.at[k, x_far], d2.at[k], s2.at[k], v2.at[k], right if to_right else left)

        def near(k, to_right):
            if to_right:
                return rc(e.at[k, x_right], l1.at[k], s1.at[k], v1.at[k], right)
            return rc(e.at[k, x_left], r1.at[k], s1.at[NZ + k], v1.at[NZ + k], left)

        def zcopy(k):
            dev = (((z + k) % NZ) * NX + x, f)
            return rc(zs.at[k], zr.at[k], sz.at[k], vz.at[k], dev)

        def start(group):
            a, b = group
            far(a, True).start()
            far(b, False).start()
            near(b, True).start()
            near(a, False).start()

        def relay(group):
            for k, to_right in zip(group, (True, False)):
                far(k, to_right).wait_recv()
                mine = x_right if to_right else x_left
                e[k, mine] = enc(dec(e[k, mine], c1) + dec(d2[k], c1), c2)
                near(k, to_right).start()

        def total(group):
            for k, relayed_right in zip(group, (True, False)):
                near(k, True).wait_recv()
                near(k, False).wait_recv()
                cl, cr = (c2, c1) if relayed_right else (c1, c2)
                part = own(k) + dec(l1[k], cl) + dec(r1[k], cr)
                if k:
                    zs[k] = enc(part, c4)
                    zcopy(k).start()
                else:
                    acc[...] = part

        def finish():
            part = acc[...]
            for k in range(1, NZ):
                zcopy(k).wait_recv()
                part = part + dec(zr[k], c4)
            acc[...] = part

        def drain():
            for a, b in GROUPS:
                far(a, True).wait_send()
                far(b, False).wait_send()
            for k in range(NZ):
                near(k, True).wait_send()
                near(k, False).wait_send()
                if k:
                    zcopy(k).wait_send()

        return start, relay, total, finish, drain

    def piece(ref, k):
        return ref[k, :, pl.ds(pl.multiple_of(x * LANES, LANES), LANES)]

    d_start, d_relay, d_total, d_finish, d_drain = reduction(
        code, decode, CODE1, CODE2, CODE4, de, dd2, dl1, dr1, dzs, dzr, dacc,
        lambda k: piece(dbuf, k), d2send, d2recv, d1send, d1recv, dzsend, dzrecv,
    )
    o_start, o_relay, o_total, o_finish, o_drain = reduction(
        plain, unplain, 1, 1, 1, oe, od2, ol1, or1, ozs, ozr, oacc,
        lambda k: oe[k, x].astype(F32), o2send, o2recv, o1send, o1recv, ozsend, ozrecv,
    )

    def d_encode(group):
        for k in group:
            d_load(k).wait()

            @pl.loop(0, chunks)
            def _(i):
                r = pl.ds(pl.multiple_of(i * STEP_ROWS, STEP_ROWS), STEP_ROWS)
                for q in range(NX):
                    de[k, q, r, :] = code(dbuf[k, r, q * LANES:(q + 1) * LANES], CODE1)

    def schedule(prepare, start, relay, total):
        prepare(GROUPS[0])
        start(GROUPS[0])
        prepare(GROUPS[1])
        start(GROUPS[1])
        for s in range(4):
            if s + 2 < 4:
                prepare(GROUPS[s + 2])
                start(GROUPS[s + 2])
            relay(GROUPS[s])
            if s:
                total(GROUPS[s - 1])
        total(GROUPS[3])

    schedule(d_encode, d_start, d_relay, d_total)

    def y_arrival(source):
        return pltpu.make_async_remote_copy(
            src_ref=xs.at[0], dst_ref=xr.at[source], send_sem=ysend.at[0], recv_sem=yrecv.at[source],
            device_id=(isl, source), device_id_type=MESH,
        )

    contract_rows = (((0,), (0,)), ((), ()))
    for step, dy in enumerate((0, 1, 3, 2)):
        first = ((y + dy) % NY) * 2
        if dy:
            y_arrival(first).wait_recv()
            y_arrival(first + 1).wait_recv()
        else:
            y_arrival(first + 1 - core).wait_recv()
        part = xr[pl.ds(first, 2)].reshape(2 * rows, BLK)
        partial = lax.dot_general(part, part, contract_rows, preferred_element_type=F32)
        if step:
            gram[...] += partial
        else:
            gram[...] = partial

    raw = gram[...]
    row_id = lax.broadcasted_iota(jnp.int32, (BLK, BLK), 0)
    col_id = lax.broadcasted_iota(jnp.int32, (BLK, BLK), 1)
    square_norm = jnp.sum(jnp.where(row_id == col_id, raw, 0.0))
    norm = jnp.sqrt(jnp.full((1, 1), square_norm, F32))
    inverse = 1.0 / (norm + EPS)
    gram1 = (raw * inverse * inverse).astype(BF16)

    def dot(a, b):
        return jnp.dot(a, b, preferred_element_type=F32)

    poly1 = (COEF_B * gram1.astype(F32) + COEF_C * dot(gram1, gram1)).astype(BF16)
    half = (COEF_A * gram1.astype(F32) + dot(gram1, poly1)).astype(BF16)
    gram2 = (COEF_A * half.astype(F32) + dot(poly1, half)).astype(BF16)
    poly2 = (COEF_B * gram2.astype(F32) + COEF_C * dot(gram2, gram2)).astype(BF16)
    both = (
        COEF_A * (poly1.astype(F32) + poly2.astype(F32)) + dot(poly1, poly2)
    ).astype(BF16)

    def orth(group):
        for k in group:
            block = xr[(z + k) % NZ]
            out = (COEF_A * COEF_A) * block.astype(F32) + dot(block, both)
            out = (out * inverse).astype(BF16)
            for q in range(NX):
                oe[k, q] = out[:, q * LANES:(q + 1) * LANES]

    schedule(orth, o_start, o_relay, o_total)
    d_finish()
    o_finish()

    swap_copy = pltpu.make_async_remote_copy(
        src_ref=tsend, dst_ref=trecv, send_sem=tsem.at[0], recv_sem=tsem.at[1],
        device_id=swap, device_id_type=MESH,
    )
    tsend[...] = oacc[...].astype(BF16)

    @pl.when(z != f)
    def _():
        swap_copy.start()
        swap_copy.wait_recv()
        oacc[...] = trecv[...].astype(F32)

    pseudo = (dacc[...] + STEP_SCALE * oacc[...]) * (1.0 / (NZ * NX))
    momentum = OUTER_BETA * om_ref[...] + pseudo
    nm_ref[...] = momentum
    nw_ref[...] = ow_ref[...] - OUTER_LR * (pseudo + OUTER_BETA * momentum)

    for j in range(NF):
        dy, c = SENDS[j]
        if dy:
            y_copy(j).wait_send()
        else:
            @pl.when(core != c)
            def _():
                y_copy(j).wait_send()
    d_drain()
    o_drain()

    @pl.when(z != f)
    def _():
        swap_copy.wait_send()


def on_device(gradient, momentum, drift, outer_weights, outer_momentum):
    rows = gradient.shape[1]
    vmem = pl.BlockSpec(memory_space=pltpu.VMEM)
    hbm = pl.BlockSpec(memory_space=pl.ANY)
    out = jax.ShapeDtypeStruct((rows, LANES), F32)

    def reduce_buffers():
        piece = (rows, LANES)
        return [
            pltpu.VMEM((NZ, NX) + piece, BF16),
            pltpu.VMEM((NZ,) + piece, BF16),
            pltpu.VMEM((NZ,) + piece, BF16),
            pltpu.VMEM((NZ,) + piece, BF16),
            pltpu.VMEM((NZ,) + piece, BF16),
            pltpu.VMEM((NZ,) + piece, BF16),
            pltpu.VMEM(piece, F32),
        ]

    def sems(n):
        return pltpu.SemaphoreType.DMA((n,))

    reduce_sems = [sems(NZ), sems(NZ), sems(2 * NZ), sems(2 * NZ), sems(NZ), sems(NZ)]
    call = pl.pallas_call(
        kernel,
        out_shape=(out, out),
        in_specs=[hbm, hbm, hbm, vmem, vmem],
        out_specs=(vmem, vmem),
        scratch_shapes=[
            pltpu.VMEM((NF, rows, BLK), BF16),
            pltpu.VMEM((NF, rows, BLK), BF16),
            pltpu.VMEM((NZ, rows, BLK), F32),
            pltpu.VMEM((NF, rows, BLK), BF16),
            pltpu.VMEM((NF, rows, BLK), BF16),
            pltpu.VMEM((BLK, BLK), F32),
            *reduce_buffers(),
            *reduce_buffers(),
            pltpu.VMEM((rows, LANES), BF16),
            pltpu.VMEM((rows, LANES), BF16),
            sems(3 * NF),
            sems(NF),
            sems(NF),
            *reduce_sems,
            *reduce_sems,
            sems(2),
        ],
        compiler_params=pltpu.CompilerParams(
            collective_id=0, has_side_effects=True, vmem_limit_bytes=56 * 2**20
        ),
        name="outer_step",
    )
    return call(gradient, momentum, drift, outer_weights, outer_momentum)


def solution(mesh):
    in_specs = (
        P("island", "fsdp", None),
        P("island", "fsdp", None),
        P("island", "fsdp", None),
        P("fsdp", "island"),
        P("fsdp", "island"),
    )
    out_specs = (P("fsdp", "island"), P("fsdp", "island"))
    return jax.shard_map(
        on_device, mesh=mesh, in_specs=in_specs, out_specs=out_specs, check_vma=False
    )
```

```python
import functools
import math

import jax
import jax.numpy as jnp
from jax import lax
from jax.experimental import pallas as pl
from jax.experimental.pallas import tpu as pltpu
from jax.sharding import PartitionSpec as P

ROWS = 2560
BLK = 512
EPS = 1e-07
COEF_A = 3.4445
COEF_B = -4.775
COEF_C = 2.0315
BETA = 0.95
OUTER_BETA = 0.9
OUTER_LR = 0.7
STEP_SCALE = 0.2 * math.sqrt(max(ROWS, BLK))

MESH = pl.DeviceIdType.MESH
F32 = jnp.float32
BF16 = jnp.bfloat16
NZ, NX, NY = 8, 4, 4
NF = 2 * NY
LANES = 128
GROUPS = ((4, 3), (5, 2), (6, 1), (7, 0))
SENDS = tuple((dy, core) for core in (0, 1) for dy in (2, 1, 3, 0))
CODE = 3.6
STEP_ROWS = 64


def kernel(
    g_hbm, m_hbm, d_hbm, out_ref,
    gbuf, mbuf, dbuf, xs, xr, gram, both, scale,
    de, dd2, dl1, dr1, dzs, dzr, dacc,
    oe, od2, ol1, or1, ozs, ozr, oacc, tsend, trecv,
    load_sem, ysend, yrecv,
    d2send, d2recv, d1send, d1recv, dzsend, dzrecv,
    o2send, o2recv, o1send, o1recv, ozsend, ozrecv, tsem,
):
    isl = lax.axis_index("island")
    f = lax.axis_index("fsdp")
    z, x = isl // NX, isl % NX
    y, core = f // 2, f % 2
    rows = g_hbm.shape[1]
    chunks = rows // STEP_ROWS
    right = (z * NX + (x + 1) % NX, f)
    left = (z * NX + (x + NX - 1) % NX, f)
    x_right, x_left, x_far = (x + 1) % NX, (x + NX - 1) % NX, (x + 2) % NX
    swap = (f * NX + x, z)

    def at_fsdp(dy, c):
        return ((y + dy) % NY) * 2 + c

    barrier = pltpu.get_barrier_semaphore()

    def greet(dev):
        pl.semaphore_signal(barrier, inc=1, device_id=dev, device_id_type=MESH)

    for d in range(1, NF):
        greet((isl, (f + d) % NF))
    for d in range(1, NZ):
        greet((((z + d) % NZ) * NX + x, f))
    greet(right)
    greet(left)

    @pl.when(z != f)
    def _():
        greet(swap)

    def g_load(j):
        cols = pl.ds(pl.multiple_of(at_fsdp(*SENDS[j]) * BLK, BLK), BLK)
        return (
            pltpu.make_async_copy(g_hbm.at[0, :, cols], gbuf.at[j], load_sem.at[j]),
            pltpu.make_async_copy(m_hbm.at[0, :, cols], mbuf.at[j], load_sem.at[NF + j]),
        )

    def d_load(k):
        cols = pl.ds(pl.multiple_of(((z + k) % NZ) * BLK, BLK), BLK)
        return pltpu.make_async_copy(d_hbm.at[0, :, cols], dbuf.at[k], load_sem.at[2 * NF + k])

    for j in range(NF):
        for copy in g_load(j):
            copy.start()

    def y_copy(j):
        dest = at_fsdp(*SENDS[j])
        return pltpu.make_async_remote_copy(
            src_ref=xs.at[j], dst_ref=xr.at[f], send_sem=ysend.at[j], recv_sem=yrecv.at[f],
            device_id=(isl, dest), device_id_type=MESH,
        )

    for j in range(NF):
        for copy in g_load(j):
            copy.wait()
        if j == NY - 1:
            for group in GROUPS:
                for k in group:
                    d_load(k).start()
        dy, c = SENDS[j]

        def nesterov(dst):
            @pl.loop(0, chunks)
            def _(i):
                r = pl.ds(pl.multiple_of(i * STEP_ROWS, STEP_ROWS), STEP_ROWS)
                grad = gbuf[j, r, :].astype(F32)
                mom = mbuf[j, r, :].astype(F32)
                dst[r, :] = (grad + BETA * (BETA * mom + grad)).astype(BF16)

        if dy:
            nesterov(xs.at[j])
            if j == 0:
                pl.semaphore_wait(barrier, NF - 1 + NZ - 1 + 2 + jnp.where(z != f, 1, 0))
            if j < NY:
                y_copy(j).start()
        else:
            @pl.when(core == c)
            def _():
                nesterov(xr.at[f])

            @pl.when(core != c)
            def _():
                nesterov(xs.at[j])
                y_copy(j).start()

    def reduction(merge, finish_with, e, d2, l1, r1, zs, zr, acc, own, s2, v2, s1, v1, sz, vz):
        def rc(src, dst, ss, rs, dev):
            return pltpu.make_async_remote_copy(
                src_ref=src, dst_ref=dst, send_sem=ss, recv_sem=rs, device_id=dev, device_id_type=MESH
            )

        def far(k, to_right):
            return rc(e.at[k, x_far], d2.at[k], s2.at[k], v2.at[k], right if to_right else left)

        def near(k, to_right):
            if to_right:
                return rc(e.at[k, x_right], l1.at[k], s1.at[k], v1.at[k], right)
            return rc(e.at[k, x_left], r1.at[k], s1.at[NZ + k], v1.at[NZ + k], left)

        def zcopy(k):
            dev = (((z + k) % NZ) * NX + x, f)
            return rc(zs.at[k], zr.at[k], sz.at[k], vz.at[k], dev)

        def start_far(group):
            far(group[0], True).start()
            far(group[1], False).start()

        def start_near(group):
            near(group[1], True).start()
            near(group[0], False).start()

        def relay(group):
            for k, to_right in zip(group, (True, False)):
                far(k, to_right).wait_recv()
                mine = x_right if to_right else x_left
                e[k, mine] = merge(own(k, mine), d2[k].astype(F32)).astype(BF16)
                near(k, to_right).start()

        def total(group):
            for k in group:
                near(k, True).wait_recv()
                near(k, False).wait_recv()
                part = merge(merge(own(k, x), l1[k].astype(F32)), r1[k].astype(F32))
                if k:
                    zs[k] = part.astype(BF16)
                    zcopy(k).start()
                else:
                    acc[...] = finish_with(part)

        def finish():
            part = acc[...]
            for k in range(1, NZ):
                zcopy(k).wait_recv()
                part = part + finish_with(zr[k].astype(F32))
            acc[...] = part

        def drain():
            for a, b in GROUPS:
                far(a, True).wait_send()
                far(b, False).wait_send()
            for k in range(NZ):
                near(k, True).wait_send()
                near(k, False).wait_send()
                if k:
                    zcopy(k).wait_send()

        def run(prepare, between):
            prepare(GROUPS[0])
            start_far(GROUPS[0])
            start_near(GROUPS[0])
            prepare(GROUPS[1])
            start_far(GROUPS[1])
            for s in range(len(GROUPS)):
                if s + 2 < len(GROUPS):
                    prepare(GROUPS[s + 2])
                relay(GROUPS[s])
                if s + 1 < len(GROUPS):
                    start_near(GROUPS[s + 1])
                if s + 2 < len(GROUPS):
                    start_far(GROUPS[s + 2])
                if s:
                    total(GROUPS[s - 1])
                between(s)
            total(GROUPS[-1])

        return run, finish, drain

    def drift_code(k, q):
        return jnp.exp(CODE * dbuf[k, :, pl.ds(pl.multiple_of(q * LANES, LANES), LANES)])

    d_run, d_finish, d_drain = reduction(
        lambda a, b: a * b, lambda v: jnp.log(v) * (1.0 / CODE),
        de, dd2, dl1, dr1, dzs, dzr, dacc, drift_code,
        d2send, d2recv, d1send, d1recv, dzsend, dzrecv,
    )
    o_run, o_finish, o_drain = reduction(
        lambda a, b: a + b, lambda v: v,
        oe, od2, ol1, or1, ozs, ozr, oacc, lambda k, q: oe[k, q].astype(F32),
        o2send, o2recv, o1send, o1recv, ozsend, ozrecv,
    )

    def d_encode(group):
        far_first, far_second = group
        for k, near_side in ((far_first, x_left), (far_second, x_right)):
            d_load(k).wait()
            de[k, x_far] = drift_code(k, x_far).astype(BF16)
            de[k, near_side] = drift_code(k, near_side).astype(BF16)

    def y_arrival(source):
        return pltpu.make_async_remote_copy(
            src_ref=xs.at[0], dst_ref=xr.at[source], send_sem=ysend.at[0], recv_sem=yrecv.at[source],
            device_id=(isl, source), device_id_type=MESH,
        )

    contract_rows = (((0,), (0,)), ((), ()))

    def dot(a, b):
        return jnp.dot(a, b, preferred_element_type=F32)

    def newton():
        for step, dy in enumerate((0, 1, 3, 2)):
            first = ((y + dy) % NY) * 2
            if dy:
                y_arrival(first).wait_recv()
                y_arrival(first + 1).wait_recv()
            else:
                y_arrival(first + 1 - core).wait_recv()
            part = xr[pl.ds(first, 2)].reshape(2 * rows, BLK)
            partial = lax.dot_general(part, part, contract_rows, preferred_element_type=F32)
            if step:
                gram[...] += partial
            else:
                gram[...] = partial
        raw = gram[...]
        row_id = lax.broadcasted_iota(jnp.int32, (BLK, BLK), 0)
        col_id = lax.broadcasted_iota(jnp.int32, (BLK, BLK), 1)
        square_norm = jnp.sum(jnp.where(row_id == col_id, raw, 0.0))
        norm = jnp.sqrt(jnp.full((1, 1), square_norm, F32))
        inverse = 1.0 / (norm + EPS)
        gram1 = (raw * inverse * inverse).astype(BF16)
        poly1 = (COEF_B * gram1.astype(F32) + COEF_C * dot(gram1, gram1)).astype(BF16)
        half = (COEF_A * gram1.astype(F32) + dot(gram1, poly1)).astype(BF16)
        gram2 = (COEF_A * half.astype(F32) + dot(poly1, half)).astype(BF16)
        poly2 = (COEF_B * gram2.astype(F32) + COEF_C * dot(gram2, gram2)).astype(BF16)
        both[...] = (
            COEF_A * (poly1.astype(F32) + poly2.astype(F32)) + dot(poly1, poly2)
        ).astype(BF16)
        scale[...] = jnp.broadcast_to(inverse, scale.shape)

    def between(s):
        if s == 2:
            for j in range(NY):
                if SENDS[j][0]:
                    y_copy(j).wait_send()
            for j in range(NY, NF):
                if SENDS[j][0]:
                    y_copy(j).start()

            @pl.when(core == 0)
            def _():
                newton()

    d_run(d_encode, between)

    @pl.when(core == 1)
    def _():
        d_finish()
        newton()

    def orth(group):
        for k in group:
            block = xr[(z + k) % NZ]
            out = (COEF_A * COEF_A) * block.astype(F32) + dot(block, both[...])
            out = (out * scale[0:1, 0:1]).astype(BF16)
            for q in range(NX):
                oe[k, q] = out[:, q * LANES:(q + 1) * LANES]

    o_run(orth, lambda s: None)

    @pl.when(core == 0)
    def _():
        d_finish()

    o_finish()

    swap_copy = pltpu.make_async_remote_copy(
        src_ref=tsend, dst_ref=trecv, send_sem=tsem.at[0], recv_sem=tsem.at[1],
        device_id=swap, device_id_type=MESH,
    )
    tsend[...] = oacc[...].astype(BF16)

    @pl.when(z != f)
    def _():
        swap_copy.start()
        swap_copy.wait_recv()
        oacc[...] = trecv[...].astype(F32)

    out_ref[...] = dacc[...] + STEP_SCALE * oacc[...]

    for j in range(NF):
        dy, c = SENDS[j]
        if dy and j >= NY:
            y_copy(j).wait_send()
        if not dy:
            @pl.when(core != c)
            def _():
                y_copy(j).wait_send()
    d_drain()
    o_drain()

    @pl.when(z != f)
    def _():
        swap_copy.wait_send()


def on_device(gradient, momentum, drift, outer_weights, outer_momentum):
    rows = gradient.shape[1]
    vmem = pl.BlockSpec(memory_space=pltpu.VMEM)
    hbm = pl.BlockSpec(memory_space=pl.ANY)
    out = jax.ShapeDtypeStruct((rows, LANES), F32)

    def reduce_buffers():
        piece = (rows, LANES)
        return [
            pltpu.VMEM((NZ, NX) + piece, BF16),
            pltpu.VMEM((NZ,) + piece, BF16),
            pltpu.VMEM((NZ,) + piece, BF16),
            pltpu.VMEM((NZ,) + piece, BF16),
            pltpu.VMEM((NZ,) + piece, BF16),
            pltpu.VMEM((NZ,) + piece, BF16),
            pltpu.VMEM(piece, F32),
        ]

    def sems(n):
        return pltpu.SemaphoreType.DMA((n,))

    reduce_sems = [sems(NZ), sems(NZ), sems(2 * NZ), sems(2 * NZ), sems(NZ), sems(NZ)]
    call = pl.pallas_call(
        kernel,
        out_shape=out,
        in_specs=[hbm, hbm, hbm],
        out_specs=vmem,
        scratch_shapes=[
            pltpu.VMEM((NF, rows, BLK), BF16),
            pltpu.VMEM((NF, rows, BLK), BF16),
            pltpu.VMEM((NZ, rows, BLK), F32),
            pltpu.VMEM((NF, rows, BLK), BF16),
            pltpu.VMEM((NF, rows, BLK), BF16),
            pltpu.VMEM((BLK, BLK), F32),
            pltpu.VMEM((BLK, BLK), BF16),
            pltpu.VMEM((8, LANES), F32),
            *reduce_buffers(),
            *reduce_buffers(),
            pltpu.VMEM((rows, LANES), BF16),
            pltpu.VMEM((rows, LANES), BF16),
            sems(3 * NF),
            sems(NF),
            sems(NF),
            *reduce_sems,
            *reduce_sems,
            sems(2),
        ],
        compiler_params=pltpu.CompilerParams(
            collective_id=0, has_side_effects=True, vmem_limit_bytes=56 * 2**20
        ),
        name="outer_step",
    )
    total = call(gradient, momentum, drift)
    pseudo = total / (NZ * NX)
    new_momentum = OUTER_BETA * outer_momentum + pseudo
    new_weights = outer_weights - OUTER_LR * (pseudo + OUTER_BETA * new_momentum)
    return (new_weights, new_momentum)


def solution(mesh):
    in_specs = (
        P("island", "fsdp", None),
        P("island", "fsdp", None),
        P("island", "fsdp", None),
        P("fsdp", "island"),
        P("fsdp", "island"),
    )
    out_specs = (P("fsdp", "island"), P("fsdp", "island"))
    return jax.shard_map(
        on_device, mesh=mesh, in_specs=in_specs, out_specs=out_specs, check_vma=False
    )
```

```python
import functools
import math

import jax
import jax.numpy as jnp
from jax import lax
from jax.experimental import pallas as pl
from jax.experimental.pallas import tpu as pltpu
from jax.sharding import PartitionSpec as P

ROWS = 2560
BLK = 512
EPS = 1e-07
COEF_A = 3.4445
COEF_B = -4.775
COEF_C = 2.0315
BETA = 0.95
OUTER_BETA = 0.9
OUTER_LR = 0.7
STEP_SCALE = 0.2 * math.sqrt(max(ROWS, BLK))

MESH = pl.DeviceIdType.MESH
F32 = jnp.float32
BF16 = jnp.bfloat16
NZ, NX, NY = 8, 4, 4
NF = 2 * NY
LANES = 128
D_PAIRS = ((4, 3), (5, 2), (6, 1), (7, 0))
O_PAIRS = ((4, 3), (5, 2), (6, 0))
FOLDED = (1, 7)
SENDS = tuple((dy, core) for core in (0, 1) for dy in (2, 1, 3, 0))
CODE = 3.6
STEP_ROWS = 64
EARLY = 2


def kernel(
    g_hbm, m_hbm, d_hbm, out_ref,
    gbuf, mbuf, dbuf, xs, xr, gram, both, scale,
    de, dd2, dl1, dr1, dzs, dzr, dacc,
    oe, od2, ol1, or1, ozs, ozr, oacc, fold, tsend, trecv,
    load_sem, ysend, yrecv,
    d2send, d2recv, d1send, d1recv, dzsend, dzrecv,
    o2send, o2recv, o1send, o1recv, ozsend, ozrecv, fold_sem, tsem,
):
    isl = lax.axis_index("island")
    f = lax.axis_index("fsdp")
    z, x = isl // NX, isl % NX
    y, core = f // 2, f % 2
    rows = g_hbm.shape[1]
    chunks = rows // STEP_ROWS
    right = (z * NX + (x + 1) % NX, f)
    left = (z * NX + (x + NX - 1) % NX, f)
    x_right, x_left, x_far = (x + 1) % NX, (x + NX - 1) % NX, (x + 2) % NX
    swap = (f * NX + x, z)

    def at_fsdp(dy, c):
        return ((y + dy) % NY) * 2 + c

    barrier = pltpu.get_barrier_semaphore()

    def greet(dev):
        pl.semaphore_signal(barrier, inc=1, device_id=dev, device_id_type=MESH)

    for d in range(1, NF):
        greet((isl, (f + d) % NF))
    for d in range(1, NZ):
        greet((((z + d) % NZ) * NX + x, f))
    greet(right)
    greet(left)

    @pl.when(z != f)
    def _():
        greet(swap)

    def g_load(j):
        cols = pl.ds(pl.multiple_of(at_fsdp(*SENDS[j]) * BLK, BLK), BLK)
        return (
            pltpu.make_async_copy(g_hbm.at[0, :, cols], gbuf.at[j], load_sem.at[j]),
            pltpu.make_async_copy(m_hbm.at[0, :, cols], mbuf.at[j], load_sem.at[NF + j]),
        )

    def d_load(k):
        cols = pl.ds(pl.multiple_of(((z + k) % NZ) * BLK, BLK), BLK)
        return pltpu.make_async_copy(d_hbm.at[0, :, cols], dbuf.at[k], load_sem.at[2 * NF + k])

    first_sends = NY - 1
    for j in range(NF):
        for copy in g_load(j):
            copy.start()
        if j == first_sends - 1:
            for k in D_PAIRS[0] + D_PAIRS[1]:
                d_load(k).start()
    for k in D_PAIRS[2] + D_PAIRS[3]:
        d_load(k).start()

    def y_copy(j):
        dest = at_fsdp(*SENDS[j])
        return pltpu.make_async_remote_copy(
            src_ref=xs.at[j], dst_ref=xr.at[f], send_sem=ysend.at[j], recv_sem=yrecv.at[f],
            device_id=(isl, dest), device_id_type=MESH,
        )

    def y_block(j):
        for copy in g_load(j):
            copy.wait()
        dy, c = SENDS[j]

        def nesterov(dst):
            @pl.loop(0, chunks)
            def _(i):
                r = pl.ds(pl.multiple_of(i * STEP_ROWS, STEP_ROWS), STEP_ROWS)
                grad = gbuf[j, r, :].astype(F32)
                mom = mbuf[j, r, :].astype(F32)
                dst[r, :] = (grad + BETA * (BETA * mom + grad)).astype(BF16)

        if dy:
            nesterov(xs.at[j])
            if j == 0:
                pl.semaphore_wait(barrier, NF - 1 + NZ - 1 + 2 + jnp.where(z != f, 1, 0))
            y_copy(j).start()
        else:
            @pl.when(core == c)
            def _():
                nesterov(xr.at[f])

            @pl.when(core != c)
            def _():
                nesterov(xs.at[j])
                y_copy(j).start()

    def reduction(groups, merge, finish_with, e, d2, l1, r1, zs, zr, acc, own, s2, v2, s1, v1, sz, vz):
        def rc(src, dst, ss, rs, dev):
            return pltpu.make_async_remote_copy(
                src_ref=src, dst_ref=dst, send_sem=ss, recv_sem=rs, device_id=dev, device_id_type=MESH
            )

        def far(k, to_right):
            return rc(e.at[k, x_far], d2.at[k], s2.at[k], v2.at[k], right if to_right else left)

        def near(k, to_right):
            if to_right:
                return rc(e.at[k, x_right], l1.at[k], s1.at[k], v1.at[k], right)
            return rc(e.at[k, x_left], r1.at[k], s1.at[NZ + k], v1.at[NZ + k], left)

        def zcopy(k):
            dev = (((z + k) % NZ) * NX + x, f)
            return rc(zs.at[k], zr.at[k], sz.at[k], vz.at[k], dev)

        over_z = [k for group in groups for k in group if k]

        goes_right = {k: n == 0 for group in groups for n, k in enumerate(group)}

        def start_far(ks):
            for k in ks:
                far(k, goes_right[k]).start()

        def start_near(ks):
            for k in ks:
                near(k, not goes_right[k]).start()

        def relay(ks):
            for k in ks:
                far(k, goes_right[k]).wait_recv()
                mine = x_right if goes_right[k] else x_left
                e[k, mine] = merge(own(k, mine), d2[k].astype(F32)).astype(BF16)
                near(k, goes_right[k]).start()

        def total(ks):
            for k in ks:
                near(k, True).wait_recv()
                near(k, False).wait_recv()
                part = merge(merge(own(k, x), l1[k].astype(F32)), r1[k].astype(F32))
                if k:
                    zs[k] = part.astype(BF16)
                    zcopy(k).start()
                else:
                    acc[...] = finish_with(part)

        def finish():
            part = acc[...]
            for k in over_z:
                zcopy(k).wait_recv()
                part = part + finish_with(zr[k].astype(F32))
            acc[...] = part

        def drain():
            for a, b in groups:
                far(a, True).wait_send()
                far(b, False).wait_send()
                for k in (a, b):
                    near(k, True).wait_send()
                    near(k, False).wait_send()
            for k in over_z:
                zcopy(k).wait_send()

        return start_far, start_near, relay, total, finish, drain

    def drift_code(k, q):
        return jnp.exp(CODE * dbuf[k, :, pl.ds(pl.multiple_of(q * LANES, LANES), LANES)])

    d_far, d_near, d_relay, d_total, d_finish, d_drain = reduction(
        D_PAIRS, lambda a, b: a * b, lambda v: jnp.log(v) * (1.0 / CODE),
        de, dd2, dl1, dr1, dzs, dzr, dacc, drift_code,
        d2send, d2recv, d1send, d1recv, dzsend, dzrecv,
    )
    o_far, o_near, o_relay, o_total, o_finish, o_drain = reduction(
        O_PAIRS, lambda a, b: a + b, lambda v: v,
        oe, od2, ol1, or1, ozs, ozr, oacc, lambda k, q: oe[k, q].astype(F32),
        o2send, o2recv, o1send, o1recv, ozsend, ozrecv,
    )

    def d_encode(group):
        far_first, far_second = group
        for k, near_side in ((far_first, x_left), (far_second, x_right)):
            d_load(k).wait()
            de[k, x_far] = drift_code(k, x_far).astype(BF16)
            de[k, near_side] = drift_code(k, near_side).astype(BF16)

    for j in range(first_sends):
        y_block(j)
    d_encode(D_PAIRS[0])
    d_far(D_PAIRS[0])
    d_near(D_PAIRS[0])
    d_encode(D_PAIRS[1])
    d_far(D_PAIRS[1])
    for j in range(first_sends, NF):
        y_block(j)

    def y_arrival(source):
        return pltpu.make_async_remote_copy(
            src_ref=xs.at[0], dst_ref=xr.at[source], send_sem=ysend.at[0], recv_sem=yrecv.at[source],
            device_id=(isl, source), device_id_type=MESH,
        )

    contract_rows = (((0,), (0,)), ((), ()))

    def dot(a, b):
        return jnp.dot(a, b, preferred_element_type=F32)

    def newton():
        for step, dy in enumerate((0, 2, 1, 3)):
            first = ((y + dy) % NY) * 2
            if dy:
                y_arrival(first).wait_recv()
                y_arrival(first + 1).wait_recv()
            else:
                y_arrival(first + 1 - core).wait_recv()
            part = xr[pl.ds(first, 2)].reshape(2 * rows, BLK)
            partial = lax.dot_general(part, part, contract_rows, preferred_element_type=F32)
            if step:
                gram[...] += partial
            else:
                gram[...] = partial
        raw = gram[...]
        row_id = lax.broadcasted_iota(jnp.int32, (BLK, BLK), 0)
        col_id = lax.broadcasted_iota(jnp.int32, (BLK, BLK), 1)
        square_norm = jnp.sum(jnp.where(row_id == col_id, raw, 0.0))
        norm = jnp.sqrt(jnp.full((1, 1), square_norm, F32))
        inverse = 1.0 / (norm + EPS)
        gram1 = (raw * inverse * inverse).astype(BF16)
        poly1 = (COEF_B * gram1.astype(F32) + COEF_C * dot(gram1, gram1)).astype(BF16)
        half = (COEF_A * gram1.astype(F32) + dot(gram1, poly1)).astype(BF16)
        gram2 = (COEF_A * half.astype(F32) + dot(poly1, half)).astype(BF16)
        poly2 = (COEF_B * gram2.astype(F32) + COEF_C * dot(gram2, gram2)).astype(BF16)
        both[...] = (
            COEF_A * (poly1.astype(F32) + poly2.astype(F32)) + dot(poly1, poly2)
        ).astype(BF16)
        scale[...] = jnp.broadcast_to(inverse, scale.shape)

    def fold_copy(n):
        k = FOLDED[n]
        return pltpu.make_async_remote_copy(
            src_ref=oe.at[k], dst_ref=fold.at[n], send_sem=fold_sem.at[n], recv_sem=fold_sem.at[2 + n],
            device_id=(((z + k) % NZ) * NX + x, f), device_id_type=MESH,
        )

    def orth(k):
        block = xr[(z + k) % NZ]
        out = (COEF_A * COEF_A) * block.astype(F32) + dot(block, both[...])
        out = (out * scale[0:1, 0:1]).astype(BF16)
        for q in range(NX):
            oe[k, q] = out[:, q * LANES:(q + 1) * LANES]

    def o_open():
        newton()
        for k in O_PAIRS[0]:
            orth(k)
            o_far((k,))
            o_near((k,))
        for n in range(len(FOLDED)):
            orth(FOLDED[n])
            fold_copy(n).start()
        for k in (5, 2, 6):
            orth(k)
            o_far((k,))
        orth(0)

    last = len(D_PAIRS) - 1
    for s in range(last + 1):
        if s + 2 <= last:
            d_encode(D_PAIRS[s + 2])
        d_relay(D_PAIRS[s])
        if s + 1 <= last:
            d_near(D_PAIRS[s + 1])
        if s + 2 <= last:
            d_far(D_PAIRS[s + 2])
        if s:
            d_total(D_PAIRS[s - 1])
        if s == EARLY:
            @pl.when(core == 0)
            def _():
                o_open()

    d_total(D_PAIRS[last])

    @pl.when(core == 1)
    def _():
        d_finish()
        o_open()

    o_relay((4, 3))
    o_near((5, 2, 6))
    o_relay((5, 2, 6))
    o_total((4, 3))
    fold_copy(0).wait_recv()
    fold_copy(1).wait_recv()
    for q in range(NX):
        oe[0, q] = (oe[0, q].astype(F32) + fold[0, q].astype(F32) + fold[1, q].astype(F32)).astype(BF16)
    o_far((0,))
    o_near((0,))
    o_total((5, 2, 6))
    o_relay((0,))
    o_total((0,))
    o_finish()

    swap_copy = pltpu.make_async_remote_copy(
        src_ref=tsend, dst_ref=trecv, send_sem=tsem.at[0], recv_sem=tsem.at[1],
        device_id=swap, device_id_type=MESH,
    )
    tsend[...] = oacc[...].astype(BF16)

    @pl.when(z != f)
    def _():
        swap_copy.start()

    @pl.when(core == 0)
    def _():
        d_finish()

    @pl.when(z != f)
    def _():
        swap_copy.wait_recv()
        oacc[...] = trecv[...].astype(F32)

    out_ref[...] = dacc[...] + STEP_SCALE * oacc[...]

    for j in range(NF):
        dy, c = SENDS[j]
        if dy:
            y_copy(j).wait_send()
        if not dy:
            @pl.when(core != c)
            def _():
                y_copy(j).wait_send()
    fold_copy(0).wait_send()
    fold_copy(1).wait_send()
    d_drain()
    o_drain()

    @pl.when(z != f)
    def _():
        swap_copy.wait_send()


def on_device(gradient, momentum, drift, outer_weights, outer_momentum):
    rows = gradient.shape[1]
    vmem = pl.BlockSpec(memory_space=pltpu.VMEM)
    hbm = pl.BlockSpec(memory_space=pl.ANY)
    out = jax.ShapeDtypeStruct((rows, LANES), F32)

    piece = (rows, LANES)
    reduce_buffers = [
        pltpu.VMEM((NZ, NX) + piece, BF16),
        *[pltpu.VMEM((NZ,) + piece, BF16)] * 5,
        pltpu.VMEM(piece, F32),
    ]

    def sems(n):
        return pltpu.SemaphoreType.DMA((n,))

    reduce_sems = [sems(NZ), sems(NZ), sems(2 * NZ), sems(2 * NZ), sems(NZ), sems(NZ)]
    call = pl.pallas_call(
        kernel,
        out_shape=out,
        in_specs=[hbm, hbm, hbm],
        out_specs=vmem,
        scratch_shapes=[
            pltpu.VMEM((NF, rows, BLK), BF16),
            pltpu.VMEM((NF, rows, BLK), BF16),
            pltpu.VMEM((NZ, rows, BLK), F32),
            pltpu.VMEM((NF, rows, BLK), BF16),
            pltpu.VMEM((NF, rows, BLK), BF16),
            pltpu.VMEM((BLK, BLK), F32),
            pltpu.VMEM((BLK, BLK), BF16),
            pltpu.VMEM((8, LANES), F32),
            *reduce_buffers,
            *reduce_buffers,
            pltpu.VMEM((len(FOLDED), NX) + piece, BF16),
            pltpu.VMEM(piece, BF16),
            pltpu.VMEM(piece, BF16),
            sems(3 * NF),
            sems(NF),
            sems(NF),
            *reduce_sems,
            *reduce_sems,
            sems(2 * len(FOLDED)),
            sems(2),
        ],
        compiler_params=pltpu.CompilerParams(
            collective_id=0, has_side_effects=True, vmem_limit_bytes=56 * 2**20
        ),
        name="outer_step",
    )
    total = call(gradient, momentum, drift)
    pseudo = total / (NZ * NX)
    new_momentum = OUTER_BETA * outer_momentum + pseudo
    new_weights = outer_weights - OUTER_LR * (pseudo + OUTER_BETA * new_momentum)
    return (new_weights, new_momentum)


def solution(mesh):
    in_specs = (
        P("island", "fsdp", None),
        P("island", "fsdp", None),
        P("island", "fsdp", None),
        P("fsdp", "island"),
        P("fsdp", "island"),
    )
    out_specs = (P("fsdp", "island"), P("fsdp", "island"))
    return jax.shard_map(
        on_device, mesh=mesh, in_specs=in_specs, out_specs=out_specs, check_vma=False
    )
```

```python
import functools
import math

import jax
import jax.numpy as jnp
from jax import lax
from jax.experimental import pallas as pl
from jax.experimental.pallas import tpu as pltpu
from jax.sharding import PartitionSpec as P

ROWS = 2560
BLK = 512
EPS = 1e-07
COEF_A = 3.4445
COEF_B = -4.775
COEF_C = 2.0315
BETA = 0.95
OUTER_BETA = 0.9
OUTER_LR = 0.7
STEP_SCALE = 0.2 * math.sqrt(max(ROWS, BLK))

MESH = pl.DeviceIdType.MESH
F32 = jnp.float32
BF16 = jnp.bfloat16
NZ, NX, NY = 8, 4, 4
NF = 2 * NY
LANES = 128
D_PAIRS = ((4, 3), (5, 2), (6, 1), (7, 0))
O_PAIRS = ((4, 3), (5, 2), (6, 0))
FOLDED = (1, 7)
SENDS = tuple((dy, core) for core in (0, 1) for dy in (2, 1, 3, 0))
CODE = 3.6
STEP_ROWS = 64
EARLY = 2


def kernel(
    g_hbm, m_hbm, d_hbm, out_ref,
    gbuf, mbuf, dbuf, xs, xr, gram, both, scale,
    de, dd2, dl1, dr1, dzs, dzr, dacc,
    oe, od2, ol1, or1, ozs, ozr, oacc, fold, tsend, trecv,
    load_sem, ysend, yrecv,
    d2send, d2recv, d1send, d1recv, dzsend, dzrecv,
    o2send, o2recv, o1send, o1recv, ozsend, ozrecv, fold_send, fold_recv, tsem,
):
    isl = lax.axis_index("island")
    f = lax.axis_index("fsdp")
    z, x = isl // NX, isl % NX
    y, core = f // 2, f % 2
    rows = g_hbm.shape[1]
    chunks = rows // STEP_ROWS
    right = (z * NX + (x + 1) % NX, f)
    left = (z * NX + (x + NX - 1) % NX, f)
    x_right, x_left, x_far = (x + 1) % NX, (x + NX - 1) % NX, (x + 2) % NX
    swap = (f * NX + x, z)

    def at_fsdp(dy, c):
        return ((y + dy) % NY) * 2 + c

    barrier = pltpu.get_barrier_semaphore()

    def greet(dev):
        pl.semaphore_signal(barrier, inc=1, device_id=dev, device_id_type=MESH)

    for d in range(1, NF):
        greet((isl, (f + d) % NF))
    for d in range(1, NZ):
        greet((((z + d) % NZ) * NX + x, f))
    greet(right)
    greet(left)

    @pl.when(z != f)
    def _():
        greet(swap)

    def g_load(j):
        cols = pl.ds(pl.multiple_of(at_fsdp(*SENDS[j]) * BLK, BLK), BLK)
        return (
            pltpu.make_async_copy(g_hbm.at[0, :, cols], gbuf.at[j], load_sem.at[j]),
            pltpu.make_async_copy(m_hbm.at[0, :, cols], mbuf.at[j], load_sem.at[NF + j]),
        )

    def d_load(k):
        cols = pl.ds(pl.multiple_of(((z + k) % NZ) * BLK, BLK), BLK)
        return pltpu.make_async_copy(d_hbm.at[0, :, cols], dbuf.at[k], load_sem.at[2 * NF + k])

    first_sends = NY - 1
    for j in range(NF):
        for copy in g_load(j):
            copy.start()
        if j == first_sends - 1:
            for k in D_PAIRS[0] + D_PAIRS[1]:
                d_load(k).start()
    for k in D_PAIRS[2] + D_PAIRS[3]:
        d_load(k).start()

    def y_copy(j):
        dest = at_fsdp(*SENDS[j])
        return pltpu.make_async_remote_copy(
            src_ref=xs.at[j], dst_ref=xr.at[f], send_sem=ysend.at[j], recv_sem=yrecv.at[f],
            device_id=(isl, dest), device_id_type=MESH,
        )

    def y_block(j):
        for copy in g_load(j):
            copy.wait()
        dy, c = SENDS[j]

        def nesterov(dst):
            @pl.loop(0, chunks)
            def _(i):
                r = pl.ds(pl.multiple_of(i * STEP_ROWS, STEP_ROWS), STEP_ROWS)
                grad = gbuf[j, r, :].astype(F32)
                mom = mbuf[j, r, :].astype(F32)
                dst[r, :] = (grad + BETA * (BETA * mom + grad)).astype(BF16)

        if dy:
            nesterov(xs.at[j])
            if j == 0:
                pl.semaphore_wait(barrier, NF - 1 + NZ - 1 + 2 + jnp.where(z != f, 1, 0))
            y_copy(j).start()
        else:
            @pl.when(core == c)
            def _():
                nesterov(xr.at[f])

            @pl.when(core != c)
            def _():
                nesterov(xs.at[j])
                y_copy(j).start()

    def reduction(groups, merge, finish_with, e, d2, l1, r1, zs, zr, acc, own, s2, v2, s1, v1, sz, vz):
        def rc(src, dst, ss, rs, dev):
            return pltpu.make_async_remote_copy(
                src_ref=src, dst_ref=dst, send_sem=ss, recv_sem=rs, device_id=dev, device_id_type=MESH
            )

        def far(k, to_right):
            return rc(e.at[k, x_far], d2.at[k], s2.at[k], v2.at[k], right if to_right else left)

        def near(k, to_right):
            if to_right:
                return rc(e.at[k, x_right], l1.at[k], s1.at[k], v1.at[k], right)
            return rc(e.at[k, x_left], r1.at[k], s1.at[NZ + k], v1.at[NZ + k], left)

        def zcopy(k):
            dev = (((z + k) % NZ) * NX + x, f)
            return rc(zs.at[k], zr.at[k], sz.at[k], vz.at[k], dev)

        over_z = [k for group in groups for k in group if k]

        goes_right = {k: n == 0 for group in groups for n, k in enumerate(group)}

        def start_far(ks):
            for k in ks:
                far(k, goes_right[k]).start()

        def start_near(ks):
            for k in ks:
                near(k, not goes_right[k]).start()

        def relay(ks):
            for k in ks:
                far(k, goes_right[k]).wait_recv()
                mine = x_right if goes_right[k] else x_left
                e[k, mine] = merge(own(k, mine), d2[k].astype(F32)).astype(BF16)
                near(k, goes_right[k]).start()

        def total(ks):
            for k in ks:
                near(k, True).wait_recv()
                near(k, False).wait_recv()
                part = merge(merge(own(k, x), l1[k].astype(F32)), r1[k].astype(F32))
                if k:
                    zs[k] = part.astype(BF16)
                    zcopy(k).start()
                else:
                    acc[...] = finish_with(part)

        def finish():
            part = acc[...]
            for k in over_z:
                zcopy(k).wait_recv()
                part = part + finish_with(zr[k].astype(F32))
            acc[...] = part

        def drain():
            for a, b in groups:
                far(a, True).wait_send()
                far(b, False).wait_send()
                for k in (a, b):
                    near(k, True).wait_send()
                    near(k, False).wait_send()
            for k in over_z:
                zcopy(k).wait_send()

        return start_far, start_near, relay, total, finish, drain

    def drift_code(k, q):
        return jnp.exp(CODE * dbuf[k, :, pl.ds(pl.multiple_of(q * LANES, LANES), LANES)])

    d_far, d_near, d_relay, d_total, d_finish, d_drain = reduction(
        D_PAIRS, lambda a, b: a * b, lambda v: jnp.log(v) * (1.0 / CODE),
        de, dd2, dl1, dr1, dzs, dzr, dacc, drift_code,
        d2send, d2recv, d1send, d1recv, dzsend, dzrecv,
    )
    o_far, o_near, o_relay, o_total, o_finish, o_drain = reduction(
        O_PAIRS, lambda a, b: a + b, lambda v: v,
        oe, od2, ol1, or1, ozs, ozr, oacc, lambda k, q: oe[k, q].astype(F32),
        o2send, o2recv, o1send, o1recv, ozsend, ozrecv,
    )

    def d_encode(group):
        far_first, far_second = group
        for k, near_side in ((far_first, x_left), (far_second, x_right)):
            d_load(k).wait()
            de[k, x_far] = drift_code(k, x_far).astype(BF16)
            de[k, near_side] = drift_code(k, near_side).astype(BF16)

    for j in range(first_sends):
        y_block(j)
    d_encode(D_PAIRS[0])
    d_far(D_PAIRS[0])
    d_near(D_PAIRS[0])
    d_encode(D_PAIRS[1])
    d_far(D_PAIRS[1])
    for j in range(first_sends, NF):
        y_block(j)

    def y_arrival(source):
        return pltpu.make_async_remote_copy(
            src_ref=xs.at[0], dst_ref=xr.at[source], send_sem=ysend.at[0], recv_sem=yrecv.at[source],
            device_id=(isl, source), device_id_type=MESH,
        )

    contract_rows = (((0,), (0,)), ((), ()))

    def dot(a, b):
        return jnp.dot(a, b, preferred_element_type=F32)

    def newton():
        for step, dy in enumerate((0, 2, 1, 3)):
            first = ((y + dy) % NY) * 2
            if dy:
                y_arrival(first).wait_recv()
                y_arrival(first + 1).wait_recv()
            else:
                y_arrival(first + 1 - core).wait_recv()
            part = xr[pl.ds(first, 2)].reshape(2 * rows, BLK)
            partial = lax.dot_general(part, part, contract_rows, preferred_element_type=F32)
            if step:
                gram[...] += partial
            else:
                gram[...] = partial
        raw = gram[...]
        row_id = lax.broadcasted_iota(jnp.int32, (BLK, BLK), 0)
        col_id = lax.broadcasted_iota(jnp.int32, (BLK, BLK), 1)
        square_norm = jnp.sum(jnp.where(row_id == col_id, raw, 0.0))
        norm = jnp.sqrt(jnp.full((1, 1), square_norm, F32))
        inverse = 1.0 / (norm + EPS)
        gram1 = (raw * inverse * inverse).astype(BF16)
        poly1 = (COEF_B * gram1.astype(F32) + COEF_C * dot(gram1, gram1)).astype(BF16)
        half = (COEF_A * gram1.astype(F32) + dot(gram1, poly1)).astype(BF16)
        gram2 = (COEF_A * half.astype(F32) + dot(poly1, half)).astype(BF16)
        poly2 = (COEF_B * gram2.astype(F32) + COEF_C * dot(gram2, gram2)).astype(BF16)
        both[...] = (
            COEF_A * (poly1.astype(F32) + poly2.astype(F32)) + dot(poly1, poly2)
        ).astype(BF16)
        scale[...] = jnp.broadcast_to(inverse, scale.shape)

    fold_order = (x_far, x_right, x_left, x)

    def fold_copy(n, i):
        k, q = FOLDED[n], fold_order[i]
        return pltpu.make_async_remote_copy(
            src_ref=oe.at[k, q], dst_ref=fold.at[n, q],
            send_sem=fold_send.at[NX * n + i], recv_sem=fold_recv.at[NX * n + i],
            device_id=(((z + k) % NZ) * NX + x, f), device_id_type=MESH,
        )

    def fold_in(i):
        q = fold_order[i]
        fold_copy(0, i).wait_recv()
        fold_copy(1, i).wait_recv()
        oe[0, q] = (oe[0, q].astype(F32) + fold[0, q].astype(F32) + fold[1, q].astype(F32)).astype(BF16)

    def orth(k):
        block = xr[(z + k) % NZ]
        out = (COEF_A * COEF_A) * block.astype(F32) + dot(block, both[...])
        out = (out * scale[0:1, 0:1]).astype(BF16)
        for q in range(NX):
            oe[k, q] = out[:, q * LANES:(q + 1) * LANES]

    def o_open():
        newton()
        for n in range(len(FOLDED)):
            orth(FOLDED[n])
            for i in range(NX):
                fold_copy(n, i).start()
        for k in O_PAIRS[0]:
            orth(k)
            o_far((k,))
            o_near((k,))
        for k in (5, 2, 6):
            orth(k)
            o_far((k,))
        orth(0)

    last = len(D_PAIRS) - 1
    for s in range(last + 1):
        if s + 2 <= last:
            d_encode(D_PAIRS[s + 2])
        d_relay(D_PAIRS[s])
        if s + 1 <= last:
            d_near(D_PAIRS[s + 1])
        if s + 2 <= last:
            d_far(D_PAIRS[s + 2])
        if s:
            d_total(D_PAIRS[s - 1])
        if s == EARLY:
            @pl.when(core == 0)
            def _():
                o_open()

    d_total(D_PAIRS[last])

    @pl.when(core == 1)
    def _():
        d_finish()
        o_open()

    o_relay((4, 3))
    o_near((5, 2))
    fold_in(0)
    o_far((0,))
    o_near((6,))
    o_relay((5, 2, 6))
    o_total((4, 3))
    fold_in(1)
    o_near((0,))
    fold_in(2)
    o_relay((0,))
    o_total((5, 2, 6))
    fold_in(3)
    o_total((0,))
    o_finish()

    swap_copy = pltpu.make_async_remote_copy(
        src_ref=tsend, dst_ref=trecv, send_sem=tsem.at[0], recv_sem=tsem.at[1],
        device_id=swap, device_id_type=MESH,
    )
    tsend[...] = oacc[...].astype(BF16)

    @pl.when(z != f)
    def _():
        swap_copy.start()

    @pl.when(core == 0)
    def _():
        d_finish()

    @pl.when(z != f)
    def _():
        swap_copy.wait_recv()
        oacc[...] = trecv[...].astype(F32)

    out_ref[...] = dacc[...] + STEP_SCALE * oacc[...]

    for j in range(NF):
        dy, c = SENDS[j]
        if dy:
            y_copy(j).wait_send()
        if not dy:
            @pl.when(core != c)
            def _():
                y_copy(j).wait_send()
    for n in range(len(FOLDED)):
        for i in range(NX):
            fold_copy(n, i).wait_send()
    d_drain()
    o_drain()

    @pl.when(z != f)
    def _():
        swap_copy.wait_send()


def on_device(gradient, momentum, drift, outer_weights, outer_momentum):
    rows = gradient.shape[1]
    vmem = pl.BlockSpec(memory_space=pltpu.VMEM)
    hbm = pl.BlockSpec(memory_space=pl.ANY)
    out = jax.ShapeDtypeStruct((rows, LANES), F32)

    piece = (rows, LANES)
    reduce_buffers = [
        pltpu.VMEM((NZ, NX) + piece, BF16),
        *[pltpu.VMEM((NZ,) + piece, BF16)] * 5,
        pltpu.VMEM(piece, F32),
    ]

    def sems(n):
        return pltpu.SemaphoreType.DMA((n,))

    reduce_sems = [sems(NZ), sems(NZ), sems(2 * NZ), sems(2 * NZ), sems(NZ), sems(NZ)]
    call = pl.pallas_call(
        kernel,
        out_shape=out,
        in_specs=[hbm, hbm, hbm],
        out_specs=vmem,
        scratch_shapes=[
            pltpu.VMEM((NF, rows, BLK), BF16),
            pltpu.VMEM((NF, rows, BLK), BF16),
            pltpu.VMEM((NZ, rows, BLK), F32),
            pltpu.VMEM((NF, rows, BLK), BF16),
            pltpu.VMEM((NF, rows, BLK), BF16),
            pltpu.VMEM((BLK, BLK), F32),
            pltpu.VMEM((BLK, BLK), BF16),
            pltpu.VMEM((8, LANES), F32),
            *reduce_buffers,
            *reduce_buffers,
            pltpu.VMEM((len(FOLDED), NX) + piece, BF16),
            pltpu.VMEM(piece, BF16),
            pltpu.VMEM(piece, BF16),
            sems(3 * NF),
            sems(NF),
            sems(NF),
            *reduce_sems,
            *reduce_sems,
            sems(len(FOLDED) * NX),
            sems(len(FOLDED) * NX),
            sems(2),
        ],
        compiler_params=pltpu.CompilerParams(
            collective_id=0, has_side_effects=True, vmem_limit_bytes=56 * 2**20
        ),
        name="outer_step",
    )
    total = call(gradient, momentum, drift)
    pseudo = total / (NZ * NX)
    new_momentum = OUTER_BETA * outer_momentum + pseudo
    new_weights = outer_weights - OUTER_LR * (pseudo + OUTER_BETA * new_momentum)
    return (new_weights, new_momentum)


def solution(mesh):
    in_specs = (
        P("island", "fsdp", None),
        P("island", "fsdp", None),
        P("island", "fsdp", None),
        P("fsdp", "island"),
        P("fsdp", "island"),
    )
    out_specs = (P("fsdp", "island"), P("fsdp", "island"))
    return jax.shard_map(
        on_device, mesh=mesh, in_specs=in_specs, out_specs=out_specs, check_vma=False
    )
```

```python
import functools
import math

import jax
import jax.numpy as jnp
from jax import lax
from jax.experimental import pallas as pl
from jax.experimental.pallas import tpu as pltpu
from jax.sharding import PartitionSpec as P

ROWS = 2560
BLK = 512
EPS = 1e-07
COEF_A = 3.4445
COEF_B = -4.775
COEF_C = 2.0315
BETA = 0.95
OUTER_BETA = 0.9
OUTER_LR = 0.7
STEP_SCALE = 0.2 * math.sqrt(max(ROWS, BLK))

MESH = pl.DeviceIdType.MESH
F32 = jnp.float32
BF16 = jnp.bfloat16
NZ, NX, NY = 8, 4, 4
NF = 2 * NY
LANES = 128
D_PAIRS = ((4, 3), (5, 2), (6, 1), (7, 0))
O_PAIRS = ((4, 3), (5, 2), (6, 0))
FOLDED = (1, 7)
SENDS = tuple((dy, core) for core in (0, 1) for dy in (2, 1, 3, 0))
CODE = 3.6
STEP_ROWS = 64
EARLY = 2


def kernel(
    g_hbm, m_hbm, d_hbm, out_ref,
    gbuf, mbuf, dbuf, xs, xr, gram, both, scale,
    de, dd2, dl1, dr1, dzs, dzr, dacc,
    oe, od2, ol1, or1, ozs, ozr, oacc, fold, tsend, trecv,
    load_sem, ysend, yrecv,
    d2send, d2recv, d1send, d1recv, dzsend, dzrecv,
    o2send, o2recv, o1send, o1recv, ozsend, ozrecv, fold_send, fold_recv, tsem,
):
    isl = lax.axis_index("island")
    f = lax.axis_index("fsdp")
    z, x = isl // NX, isl % NX
    y, core = f // 2, f % 2
    rows = g_hbm.shape[1]
    chunks = rows // STEP_ROWS
    right = (z * NX + (x + 1) % NX, f)
    left = (z * NX + (x + NX - 1) % NX, f)
    x_right, x_left, x_far = (x + 1) % NX, (x + NX - 1) % NX, (x + 2) % NX
    swap = (f * NX + x, z)

    def at_fsdp(dy, c):
        return ((y + dy) % NY) * 2 + c

    barrier = pltpu.get_barrier_semaphore()

    def greet(dev):
        pl.semaphore_signal(barrier, inc=1, device_id=dev, device_id_type=MESH)

    for d in range(1, NF):
        greet((isl, (f + d) % NF))
    for d in range(1, NZ):
        greet((((z + d) % NZ) * NX + x, f))
    greet(right)
    greet(left)

    @pl.when(z != f)
    def _():
        greet(swap)

    def g_load(j):
        cols = pl.ds(pl.multiple_of(at_fsdp(*SENDS[j]) * BLK, BLK), BLK)
        return (
            pltpu.make_async_copy(g_hbm.at[0, :, cols], gbuf.at[j], load_sem.at[j]),
            pltpu.make_async_copy(m_hbm.at[0, :, cols], mbuf.at[j], load_sem.at[NF + j]),
        )

    def d_load(k):
        cols = pl.ds(pl.multiple_of(((z + k) % NZ) * BLK, BLK), BLK)
        return pltpu.make_async_copy(d_hbm.at[0, :, cols], dbuf.at[k], load_sem.at[2 * NF + k])

    first_sends = NY - 1
    for j in range(NF):
        for copy in g_load(j):
            copy.start()
        if j == first_sends - 1:
            for k in D_PAIRS[0] + D_PAIRS[1]:
                d_load(k).start()
    for k in D_PAIRS[2] + D_PAIRS[3]:
        d_load(k).start()

    def y_copy(j):
        dest = at_fsdp(*SENDS[j])
        return pltpu.make_async_remote_copy(
            src_ref=xs.at[j], dst_ref=xr.at[f], send_sem=ysend.at[j], recv_sem=yrecv.at[f],
            device_id=(isl, dest), device_id_type=MESH,
        )

    def y_block(j):
        for copy in g_load(j):
            copy.wait()
        dy, c = SENDS[j]

        def nesterov(dst):
            @pl.loop(0, chunks)
            def _(i):
                r = pl.ds(pl.multiple_of(i * STEP_ROWS, STEP_ROWS), STEP_ROWS)
                grad = gbuf[j, r, :].astype(F32)
                mom = mbuf[j, r, :].astype(F32)
                dst[r, :] = (grad + BETA * (BETA * mom + grad)).astype(BF16)

        if dy:
            nesterov(xs.at[j])
            if j == 0:
                pl.semaphore_wait(barrier, NF - 1 + NZ - 1 + 2 + jnp.where(z != f, 1, 0))
            y_copy(j).start()
        else:
            @pl.when(core == c)
            def _():
                nesterov(xr.at[f])

            @pl.when(core != c)
            def _():
                nesterov(xs.at[j])
                y_copy(j).start()

    def reduction(groups, merge, finish_with, e, d2, l1, r1, zs, zr, acc, own, s2, v2, s1, v1, sz, vz):
        def rc(src, dst, ss, rs, dev):
            return pltpu.make_async_remote_copy(
                src_ref=src, dst_ref=dst, send_sem=ss, recv_sem=rs, device_id=dev, device_id_type=MESH
            )

        def far(k, to_right):
            return rc(e.at[k, x_far], d2.at[k], s2.at[k], v2.at[k], right if to_right else left)

        def near(k, to_right):
            if to_right:
                return rc(e.at[k, x_right], l1.at[k], s1.at[k], v1.at[k], right)
            return rc(e.at[k, x_left], r1.at[k], s1.at[NZ + k], v1.at[NZ + k], left)

        def zcopy(k):
            dev = (((z + k) % NZ) * NX + x, f)
            return rc(zs.at[k], zr.at[k], sz.at[k], vz.at[k], dev)

        over_z = [k for group in groups for k in group if k]

        goes_right = {k: n == 0 for group in groups for n, k in enumerate(group)}

        def start_far(ks):
            for k in ks:
                far(k, goes_right[k]).start()

        def start_near(ks):
            for k in ks:
                near(k, not goes_right[k]).start()

        def relay(ks):
            for k in ks:
                far(k, goes_right[k]).wait_recv()
                mine = x_right if goes_right[k] else x_left
                e[k, mine] = merge(own(k, mine), d2[k].astype(F32)).astype(BF16)
                near(k, goes_right[k]).start()

        def total(ks):
            for k in ks:
                near(k, True).wait_recv()
                near(k, False).wait_recv()
                part = merge(merge(own(k, x), l1[k].astype(F32)), r1[k].astype(F32))
                if k:
                    zs[k] = part.astype(BF16)
                    zcopy(k).start()
                else:
                    acc[...] = finish_with(part)

        def gather(ks):
            for k in ks:
                zcopy(k).wait_recv()
            part = finish_with(zr[ks[0]].astype(F32))
            for k in ks[1:]:
                part = part + finish_with(zr[k].astype(F32))
            return part

        def finish():
            acc[...] = acc[...] + gather(over_z)

        def drain():
            for a, b in groups:
                far(a, True).wait_send()
                far(b, False).wait_send()
                for k in (a, b):
                    near(k, True).wait_send()
                    near(k, False).wait_send()
            for k in over_z:
                zcopy(k).wait_send()

        return start_far, start_near, relay, total, finish, gather, drain

    def drift_code(k, q):
        return jnp.exp(CODE * dbuf[k, :, pl.ds(pl.multiple_of(q * LANES, LANES), LANES)])

    d_far, d_near, d_relay, d_total, d_finish, _, d_drain = reduction(
        D_PAIRS, lambda a, b: a * b, lambda v: jnp.log(v) * (1.0 / CODE),
        de, dd2, dl1, dr1, dzs, dzr, dacc, drift_code,
        d2send, d2recv, d1send, d1recv, dzsend, dzrecv,
    )
    o_far, o_near, o_relay, o_total, _, o_gather, o_drain = reduction(
        O_PAIRS, lambda a, b: a + b, lambda v: v,
        oe, od2, ol1, or1, ozs, ozr, oacc, lambda k, q: oe[k, q].astype(F32),
        o2send, o2recv, o1send, o1recv, ozsend, ozrecv,
    )

    def d_encode(group):
        far_first, far_second = group
        for k, near_side in ((far_first, x_left), (far_second, x_right)):
            d_load(k).wait()
            de[k, x_far] = drift_code(k, x_far).astype(BF16)
            de[k, near_side] = drift_code(k, near_side).astype(BF16)

    for j in range(first_sends):
        y_block(j)
    d_encode(D_PAIRS[0])
    d_far(D_PAIRS[0])
    d_near(D_PAIRS[0])
    d_encode(D_PAIRS[1])
    d_far(D_PAIRS[1])
    for j in range(first_sends, NF):
        y_block(j)

    def y_arrival(source):
        return pltpu.make_async_remote_copy(
            src_ref=xs.at[0], dst_ref=xr.at[source], send_sem=ysend.at[0], recv_sem=yrecv.at[source],
            device_id=(isl, source), device_id_type=MESH,
        )

    contract_rows = (((0,), (0,)), ((), ()))

    def dot(a, b):
        return jnp.dot(a, b, preferred_element_type=F32)

    def newton():
        for step, dy in enumerate((0, 2, 1, 3)):
            first = ((y + dy) % NY) * 2
            if dy:
                y_arrival(first).wait_recv()
                y_arrival(first + 1).wait_recv()
            else:
                y_arrival(first + 1 - core).wait_recv()
            part = xr[pl.ds(first, 2)].reshape(2 * rows, BLK)
            partial = lax.dot_general(part, part, contract_rows, preferred_element_type=F32)
            if step:
                gram[...] += partial
            else:
                gram[...] = partial
        raw = gram[...]
        row_id = lax.broadcasted_iota(jnp.int32, (BLK, BLK), 0)
        col_id = lax.broadcasted_iota(jnp.int32, (BLK, BLK), 1)
        square_norm = jnp.sum(jnp.where(row_id == col_id, raw, 0.0))
        norm = jnp.sqrt(jnp.full((1, 1), square_norm, F32))
        inverse = 1.0 / (norm + EPS)
        gram1 = (raw * inverse * inverse).astype(BF16)
        poly1 = (COEF_B * gram1.astype(F32) + COEF_C * dot(gram1, gram1)).astype(BF16)
        half = (COEF_A * gram1.astype(F32) + dot(gram1, poly1)).astype(BF16)
        gram2 = (COEF_A * half.astype(F32) + dot(poly1, half)).astype(BF16)
        poly2 = (COEF_B * gram2.astype(F32) + COEF_C * dot(gram2, gram2)).astype(BF16)
        both[...] = (
            COEF_A * (poly1.astype(F32) + poly2.astype(F32)) + dot(poly1, poly2)
        ).astype(BF16)
        scale[...] = jnp.broadcast_to(inverse, scale.shape)

    fold_order = (x_far, x_right, x_left, x)

    def fold_copy(n, i):
        k, q = FOLDED[n], fold_order[i]
        return pltpu.make_async_remote_copy(
            src_ref=oe.at[k, q], dst_ref=fold.at[n, q],
            send_sem=fold_send.at[NX * n + i], recv_sem=fold_recv.at[NX * n + i],
            device_id=(((z + k) % NZ) * NX + x, f), device_id_type=MESH,
        )

    def fold_in(i):
        q = fold_order[i]
        fold_copy(0, i).wait_recv()
        fold_copy(1, i).wait_recv()
        oe[0, q] = (oe[0, q].astype(F32) + fold[0, q].astype(F32) + fold[1, q].astype(F32)).astype(BF16)

    def orth(k):
        block = xr[(z + k) % NZ]
        out = (COEF_A * COEF_A) * block.astype(F32) + dot(block, both[...])
        out = (out * scale[0:1, 0:1]).astype(BF16)
        for q in range(NX):
            oe[k, q] = out[:, q * LANES:(q + 1) * LANES]

    def o_open():
        newton()
        for n in range(len(FOLDED)):
            orth(FOLDED[n])
            for i in range(NX):
                fold_copy(n, i).start()
        for k in O_PAIRS[0]:
            orth(k)
            o_far((k,))
            o_near((k,))
        for k in (5, 2, 6):
            orth(k)
            o_far((k,))
        orth(0)

    last = len(D_PAIRS) - 1
    for s in range(last + 1):
        if s + 2 <= last:
            d_encode(D_PAIRS[s + 2])
        d_relay(D_PAIRS[s])
        if s + 1 <= last:
            d_near(D_PAIRS[s + 1])
        if s + 2 <= last:
            d_far(D_PAIRS[s + 2])
        if s:
            d_total(D_PAIRS[s - 1])
        if s == EARLY:
            @pl.when(core == 0)
            def _():
                o_open()

    d_total(D_PAIRS[last])

    @pl.when(core == 1)
    def _():
        d_finish()
        o_open()

    o_relay((4, 3))
    o_near((5, 2))
    fold_in(0)
    o_far((0,))
    o_near((6,))
    o_relay((5, 2, 6))
    o_total((4, 3))
    fold_in(1)
    o_near((0,))
    fold_in(2)
    o_relay((0,))
    o_total((5, 2, 6))
    fold_in(3)
    early = o_gather((4, 3))
    o_total((0,))
    oacc[...] = oacc[...] + early + o_gather((5, 2, 6))

    swap_copy = pltpu.make_async_remote_copy(
        src_ref=tsend, dst_ref=trecv, send_sem=tsem.at[0], recv_sem=tsem.at[1],
        device_id=swap, device_id_type=MESH,
    )
    tsend[...] = oacc[...].astype(BF16)

    @pl.when(z != f)
    def _():
        swap_copy.start()

    @pl.when(core == 0)
    def _():
        d_finish()

    @pl.when(z != f)
    def _():
        swap_copy.wait_recv()
        oacc[...] = trecv[...].astype(F32)

    out_ref[...] = dacc[...] + STEP_SCALE * oacc[...]

    for j in range(NF):
        dy, c = SENDS[j]
        if dy:
            y_copy(j).wait_send()
        if not dy:
            @pl.when(core != c)
            def _():
                y_copy(j).wait_send()
    for n in range(len(FOLDED)):
        for i in range(NX):
            fold_copy(n, i).wait_send()
    d_drain()
    o_drain()

    @pl.when(z != f)
    def _():
        swap_copy.wait_send()


def on_device(gradient, momentum, drift, outer_weights, outer_momentum):
    rows = gradient.shape[1]
    vmem = pl.BlockSpec(memory_space=pltpu.VMEM)
    hbm = pl.BlockSpec(memory_space=pl.ANY)
    out = jax.ShapeDtypeStruct((rows, LANES), F32)

    piece = (rows, LANES)
    reduce_buffers = [
        pltpu.VMEM((NZ, NX) + piece, BF16),
        *[pltpu.VMEM((NZ,) + piece, BF16)] * 5,
        pltpu.VMEM(piece, F32),
    ]

    def sems(n):
        return pltpu.SemaphoreType.DMA((n,))

    reduce_sems = [sems(NZ), sems(NZ), sems(2 * NZ), sems(2 * NZ), sems(NZ), sems(NZ)]
    call = pl.pallas_call(
        kernel,
        out_shape=out,
        in_specs=[hbm, hbm, hbm],
        out_specs=vmem,
        scratch_shapes=[
            pltpu.VMEM((NF, rows, BLK), BF16),
            pltpu.VMEM((NF, rows, BLK), BF16),
            pltpu.VMEM((NZ, rows, BLK), F32),
            pltpu.VMEM((NF, rows, BLK), BF16),
            pltpu.VMEM((NF, rows, BLK), BF16),
            pltpu.VMEM((BLK, BLK), F32),
            pltpu.VMEM((BLK, BLK), BF16),
            pltpu.VMEM((8, LANES), F32),
            *reduce_buffers,
            *reduce_buffers,
            pltpu.VMEM((len(FOLDED), NX) + piece, BF16),
            pltpu.VMEM(piece, BF16),
            pltpu.VMEM(piece, BF16),
            sems(3 * NF),
            sems(NF),
            sems(NF),
            *reduce_sems,
            *reduce_sems,
            sems(len(FOLDED) * NX),
            sems(len(FOLDED) * NX),
            sems(2),
        ],
        compiler_params=pltpu.CompilerParams(
            collective_id=0, has_side_effects=True, vmem_limit_bytes=56 * 2**20
        ),
        name="outer_step",
    )
    total = call(gradient, momentum, drift)
    pseudo = total / (NZ * NX)
    new_momentum = OUTER_BETA * outer_momentum + pseudo
    new_weights = outer_weights - OUTER_LR * (pseudo + OUTER_BETA * new_momentum)
    return (new_weights, new_momentum)


def solution(mesh):
    in_specs = (
        P("island", "fsdp", None),
        P("island", "fsdp", None),
        P("island", "fsdp", None),
        P("fsdp", "island"),
        P("fsdp", "island"),
    )
    out_specs = (P("fsdp", "island"), P("fsdp", "island"))
    return jax.shard_map(
        on_device, mesh=mesh, in_specs=in_specs, out_specs=out_specs, check_vma=False
    )
```
